128 devices in a mesh: cmp: 4 (over z_lo, core), task: 32 (over x, z_hi, y).
Axes of the slice: x: 4, y: 4, z: 4 (z_hi: 2, z_lo: 2; z = z_hi * 2 + z_lo), core: 2. Of those that a mesh axis runs over, the one named last changes fastest.
Arguments:
- features: bfloat16 [1024, 16384], P('cmp', 'task'), may hold values from 0 to 2
- w_trunk: bfloat16 [16384, 4096], P('task', 'cmp'), may hold values from -0.046875 to 0.046875
- w_head: bfloat16 [4096, 65536], P(None, 'task'), may hold values from -0.09375 to 0.09375
- bias_trunk: float32 [4096], replicated, may hold values from -3 to 3
- bias_head: float32 [65536], P('task'), may hold values from -4 to 4
- targets: bfloat16 [1024, 65536], P('cmp', 'task'), may hold values from 0 to 1
- block_mask: int32 [2, 128], replicated, may hold values from 0 to 1, as said below
Outputs:
- grad_trunk: float32 [16384, 4096], P('task', 'cmp')
- grad_head: bfloat16 [4096, 65536], P('cmp', 'task')
The draws below stay inside these ranges and needn't reach their ends.
Inputs may be any that keep to these rules, and one draw needn't show every extreme that they name: `block_mask`: each entry is 0 or 1; entry [0, 0] is 1 and the last entry is 0.
All inputs are finite; a program needn't handle non-finite values.
Results may differ from the reference program's by a relative error of at most 0.011.
Values may be sent and summed in bfloat16 or wider, within the bound.
A program may use at most 128 MiB of HBM per device.

```python
import jax
import jax.numpy as jnp
from jax import lax

FP = 16384
HID = 4096
TASK_DEV = 2048
BLOCK = 512
COMPOUNDS = 1024
TASKS = 65536
CBLOCKS = 2
TBLOCKS = 128


def draw_block_mask(key, part):
    key = jax.random.fold_in(key, 7)
    first, second = jax.random.split(key)
    per_group = TASK_DEV // BLOCK
    level = jax.random.randint(first, (TBLOCKS // per_group,), 0, 4)
    level = jnp.repeat(level, per_group)
    draws = jax.random.randint(second, (CBLOCKS, TBLOCKS), 0, 8)
    mask = (draws < jnp.right_shift(8, level)[None, :]).astype(jnp.int32)
    mask = mask.at[0, 0].set(1)
    mask = mask.at[CBLOCKS - 1, TBLOCKS - 1].set(0)
    return mask


def block_levels(rng, extent, shards, least, high):
    level = 1.0
    for axis_at, blocks in shards:
        steps = jax.random.uniform(jax.random.fold_in(jax.random.fold_in(rng, 6), axis_at), (blocks,), jnp.float32, least / len(shards), high / len(shards))
        level = level * jnp.repeat(jnp.exp(steps), extent[axis_at] // blocks).reshape((-1,) + (1,) * (len(extent) - 1 - axis_at))
    return level


def scatter_about(stream_key, dims, scale, reach, cuts=(), kind=jnp.bfloat16):
    drawn = scale * jax.random.normal(stream_key, dims, jnp.float32)
    if cuts:
        drawn = drawn * block_levels(stream_key, dims, cuts, -0.22, 0.18)
    return jnp.clip(drawn, -reach, reach).astype(kind)


def setup_inputs(seed: int = 0) -> dict:
    key_of = jax.random.split(jax.random.key(seed), 8)
    return {
        "features": jnp.clip(2.0 * jax.random.uniform(key_of[0], (COMPOUNDS, FP), jnp.float32) ** block_levels(key_of[0], (COMPOUNDS, FP), ((0, 4), (1, 32)), -0.2, 0.2), 0.0, 2.0).astype(jnp.bfloat16),
        "w_trunk": scatter_about(key_of[1], (FP, HID), FP ** -0.5, 0.046875, ((0, 32), (1, 4))),
        "w_head": scatter_about(key_of[2], (HID, TASKS), HID ** -0.5, 0.09375, ((1, 32),)),
        "bias_trunk": scatter_about(key_of[3], (HID,), 0.5, 3.0, (), jnp.float32),
        "bias_head": scatter_about(key_of[4], (TASKS,), 1.0, 4.0, ((0, 32),), jnp.float32),
        "targets": jnp.clip(1.0 * jax.random.uniform(key_of[5], (COMPOUNDS, TASKS), jnp.float32) ** block_levels(key_of[5], (COMPOUNDS, TASKS), ((0, 4), (1, 32)), -0.2, 0.2), 0.0, 1.0).astype(jnp.bfloat16),
        "block_mask": draw_block_mask(jax.random.fold_in(key_of[7], 71), 0),
    }


def reference(features, w_trunk, w_head, bias_trunk, bias_head, targets, block_mask):
    scale = 1.0 / (COMPOUNDS ** 0.5)
    pre = jnp.dot(features, w_trunk, preferred_element_type=jnp.float32) + bias_trunk
    hidden = jnp.maximum(pre, 0.0).astype(jnp.bfloat16)
    row_block = jnp.arange(COMPOUNDS) // BLOCK
    mask_rows = block_mask[row_block, :].astype(jnp.float32)
    head_blocks = w_head.reshape(HID, TBLOCKS, BLOCK).transpose(1, 0, 2)
    bias_blocks = bias_head.reshape(TBLOCKS, BLOCK)
    target_blocks = targets.reshape(COMPOUNDS, TBLOCKS, BLOCK).transpose(1, 0, 2)

    def step(carry, items):
        weight, bias, target, mask = items

        def compute(carry):
            logits = jnp.dot(hidden, weight, preferred_element_type=jnp.float32) + bias
            grad_logits = (mask[:, None] * (jax.nn.sigmoid(logits) - target.astype(jnp.float32)) * scale).astype(jnp.bfloat16)
            carry = carry + jnp.dot(grad_logits, weight.T, preferred_element_type=jnp.float32)
            block_grad = jnp.dot(hidden.T, grad_logits, preferred_element_type=jnp.float32).astype(jnp.bfloat16)
            return carry, block_grad

        def empty(carry):
            return carry, jnp.zeros((HID, BLOCK), jnp.bfloat16)

        return lax.cond(jnp.max(mask) > 0, compute, empty, carry)

    grad_hidden, head_parts = lax.scan(step, jnp.zeros((COMPOUNDS, HID), jnp.float32), (head_blocks, bias_blocks, target_blocks, mask_rows.T))
    grad_head = head_parts.transpose(1, 0, 2).reshape(HID, TASKS)
    grad_pre = jnp.where(pre > 0, grad_hidden, 0.0).astype(jnp.bfloat16)
    grad_trunk = jnp.dot(features.T, grad_pre, preferred_element_type=jnp.float32)
    return grad_trunk, grad_head
```

```python
import jax
import jax.numpy as jnp
from jax import lax
from jax.experimental import pallas as pl
from jax.experimental.pallas import tpu as pltpu
from jax.sharding import PartitionSpec as P

BLOCK = 512
MESH = pl.DeviceIdType.MESH
BF16 = jnp.bfloat16
F32 = jnp.float32


def dot(a, b):
    return jnp.dot(a, b, preferred_element_type=F32)


def dot_t(a, b):
    return lax.dot_general(a, b, (((1,), (1,)), ((), ())), preferred_element_type=F32)


def kernel(
    feat_hbm, wt_hbm, wh_hbm, bt_ref, bh_ref, tg_hbm, mask_ref,
    gt_hbm, gh_hbm,
    wh, wt, wtt, feat, featt, tg,
    p, p_in1, p_s1, p_in2, p_s2, p_in3, pre, pieces,
    h1, h1t, h2, gl, glt,
    q, q_in1, q_s1, q_in2, q_s2, q_in3, back, gpt,
    gh, gt, ssem, rsem, lsem,
):
    c = lax.axis_index("cmp")
    t = lax.axis_index("task")
    x, zh, y = t // 8, (t // 4) % 2, t % 4
    zl, core = c // 2, c % 2
    across_z = (c + 2) % 4
    across_core = c + 1 - 2 * core

    def to_x(d):
        return {"task": ((x + d) % 4) * 8 + zh * 4 + y}

    def to_y(d):
        return {"task": x * 8 + zh * 4 + (y + d) % 4}

    def to_z():
        return {"task": x * 8 + (1 - zh) * 4 + y}

    first, second = (x, y), (y, x)
    to_first, to_second = (to_x, to_y), (to_y, to_x)

    sent = []

    def send(src, dst, device):
        i = len(sent)
        copy = pltpu.make_async_remote_copy(
            src_ref=src, dst_ref=dst, send_sem=ssem.at[i], recv_sem=rsem.at[i],
            device_id=device, device_id_type=MESH,
        )
        copy.start()
        sent.append(copy)
        return copy

    local = []

    def fetch(src, dst):
        copy = pltpu.make_async_copy(src, dst, lsem.at[len(local)])
        copy.start()
        local.append(copy)
        return copy

    def wait_recv(copies):
        for copy in copies:
            copy.wait_recv()

    get_feat = fetch(feat_hbm, feat.at[c])
    get_wt = fetch(wt_hbm, wt)
    get_tg = fetch(tg_hbm, tg)
    get_wh = fetch(wh_hbm, wh)

    barrier = pltpu.get_barrier_semaphore()
    peers = [to_x(d) for d in (1, 2, 3)] + [to_y(d) for d in (1, 2, 3)] + [to_z()]
    peers += [{"cmp": (c + d) % 4} for d in (1, 2, 3)]
    for peer in peers:
        pl.semaphore_signal(barrier, inc=1, device_id=peer, device_id_type=MESH)
    pl.semaphore_wait(barrier, len(peers))

    get_feat.wait()
    f_z = send(feat.at[c], feat.at[c], {"cmp": across_z})
    f_core = send(feat.at[c], feat.at[c], {"cmp": across_core})

    def turn_feat(slot):
        featt[slot // 2, :, pl.ds(pl.multiple_of(slot % 2 * 256, 256), 256)] = feat[slot].T

    turn_feat(c)
    get_wt.wait()

    @pl.loop(0, 4)
    def _(i):
        block = wt[:, pl.ds(pl.multiple_of(i * 256, 256), 256)].T
        wtt[i] = block.reshape(2, 4, 32, 512)

    f_core.wait_recv()
    turn_feat(across_core)

    def pre_tile(ch, i):
        if ch == 0:
            rows = wtt[i].reshape(256, 512)
        else:
            rows = wtt[:, :, i].reshape(256, 512)
        half = zl if ch == 0 else 1 - zl
        out = dot(rows, featt[half])
        if ch == 0:
            out = out.reshape(2, 4, 32, 512)
            for j in range(4):
                for z in range(2):
                    p[ch, i, j, z] = out[z, j]
        else:
            out = out.reshape(4, 2, 32, 512)
            for j in range(4):
                for z in range(2):
                    p[ch, i, j, z] = out[j, z]

    def start_reduce(ch, tile, buf, arrive):
        copies = []
        for d in (2, 1, 3, 0):
            i = (first[ch] + d) % 4
            tile(ch, i)
            if d:
                copies.append(send(buf.at[ch, i], arrive.at[ch, d - 1], to_first[ch](d)))
        return copies

    def add_first(ch, buf, arrive, total):
        @pl.loop(0, 8)
        def _(k):
            j, z = k // 2, k % 2
            value = buf[ch, first[ch], j, z].astype(F32)
            for d in range(3):
                value = value + arrive[ch, d, j, z].astype(F32)
            total[ch, j, z] = value.astype(total.dtype)

    def send_second(ch, total, arrive):
        copies = []
        for d in (2, 1, 3):
            j = (second[ch] + d) % 4
            copies.append(send(total.at[ch, j], arrive.at[ch, d - 1], to_second[ch](d)))
        return copies

    def add_second(ch, total, arrive, out):
        for z in range(2):
            value = total[ch, second[ch], z].astype(F32)
            for d in range(3):
                value = value + arrive[ch, d, z].astype(F32)
            out[ch, z] = value.astype(out.dtype)

    def finish_reduce(copies, buf, in1, s1, in2, s2, in3):
        moves = []
        for ch in range(2):
            wait_recv(copies[ch])
            add_first(ch, buf, in1, s1)
            moves.append(send_second(ch, s1, in2))
        last = []
        for ch in range(2):
            wait_recv(moves[ch])
            add_second(ch, s1, in2, s2)
            last.append(send(s2.at[ch, 1 - zh], in3.at[ch], to_z()))
        out = []
        for ch in range(2):
            last[ch].wait_recv()
            out.append(s2[ch, zh].astype(F32) + in3[ch].astype(F32))
        return out

    def gather_z(ch, buf):
        part = buf.at[ch, first[ch], second[ch], zh]
        return send(part, part, to_z())

    def gather_second(ch, buf):
        part = buf.at[ch, first[ch], second[ch]]
        return [send(part, part, to_second[ch](d)) for d in (2, 1, 3)]

    def gather_first(ch, buf):
        part = buf.at[ch, first[ch]]
        return [send(part, part, to_first[ch](d)) for d in (2, 1, 3)]

    moving0 = start_reduce(0, pre_tile, p, p_in1)
    f_z.wait_recv()
    f_far = send(feat.at[across_z], feat.at[across_z], {"cmp": across_core})
    turn_feat(across_z)
    f_far.wait_recv()
    turn_feat((across_core + 2) % 4)
    moving1 = start_reduce(1, pre_tile, p, p_in1)
    sums = finish_reduce([moving0, moving1], p, p_in1, p_s1, p_in2, p_s2, p_in3)

    row = bt_ref[pl.ds(c * 8 + t // 4, 1), :]
    lane = lax.broadcasted_iota(jnp.int32, (32, 128), 1)
    unit = lax.broadcasted_iota(jnp.int32, (32, 128), 0)
    bias = jnp.sum(
        jnp.where(lane == unit + (t % 4) * 32, jnp.broadcast_to(row, (32, 128)), 0.0),
        axis=1, keepdims=True,
    )
    for ch in range(2):
        half = zl if ch == 0 else 1 - zl
        value = sums[ch] + bias
        pre[half] = value
        value = jnp.maximum(value, 0.0).astype(BF16)
        h2[half, first_of(half, x, y), second_of(half, x, y), zh] = value
        pieces[2 * half] = value[:, :256]
        pieces[2 * half + 1] = value[:, 256:]
    own = c // 2
    slot = h1.at[own, first_of(own, x, y), second_of(own, x, y), zh, core]
    swap = []
    for d in (2, 1, 3):
        swap.append(send(pieces.at[(c + d) % 4], slot, {"cmp": (c + d) % 4}))
    h1[own, first_of(own, x, y), second_of(own, x, y), zh, core] = pieces[c]
    g2z = [gather_z(ch, h2) for ch in range(2)]
    wait_recv(swap)

    g1z = [gather_z(ch, h1) for ch in range(2)]
    g1s = []
    for ch in range(2):
        g1z[ch].wait_recv()
        g1s.append(gather_second(ch, h1))
    g1f = []
    for ch in range(2):
        wait_recv(g1s[ch])
        g1f.append(gather_first(ch, h1))
    g2s = []
    for ch in range(2):
        g2z[ch].wait_recv()
        g2s.append(gather_second(ch, h2))
    for ch in range(2):
        wait_recv(g1f[ch])
    g2f = []
    for ch in range(2):
        wait_recv(g2s[ch])
        g2f.append(gather_first(ch, h2))

    for ch in range(2):
        @pl.loop(0, 8)
        def _(k):
            quarter, i = k // 4, k % 4
            if ch == 0:
                parts = [h1[ch, i, j, z, quarter] for z in range(2) for j in range(4)]
            else:
                parts = [h1[ch, j, i, z, quarter] for z in range(2) for j in range(4)]
            block = jnp.concatenate(parts, axis=0)
            column = pl.multiple_of(ch * 2048 + quarter * 1024 + i * 256, 256)
            h1t[:, pl.ds(column, 256)] = block.T

    get_wh.wait()
    get_tg.wait()

    @pl.loop(0, 4)
    def _(k):
        cols = pl.ds(pl.multiple_of(k * BLOCK, BLOCK), BLOCK)
        logits = dot(h1t[...], wh[:, :, :, :, :, cols].reshape(4096, BLOCK)) + bh_ref[:, cols]
        seen = mask_ref[zl, t * 4 + k].astype(F32)
        error = seen * (jax.nn.sigmoid(logits) - tg[:, cols].astype(F32)) * (1.0 / 32.0)
        error = error.astype(BF16)
        gl[c, :, cols] = error
        glt[cols, :] = error.T

    g_z = send(gl.at[c], gl.at[c], {"cmp": across_z})
    g_core = send(gl.at[c], gl.at[c], {"cmp": across_core})

    def back_tile(ch, i):
        @pl.loop(0, 2)
        def _(quarter):
            if ch == 0:
                rows = wh[ch * 2 + quarter, i].reshape(256, 2048)
            else:
                rows = wh[ch * 2 + quarter, :, :, i].reshape(256, 2048)
            out = dot(rows, glt[...]).astype(BF16)
            if ch == 0:
                out = out.reshape(2, 4, 32, 256)
                for j in range(4):
                    for z in range(2):
                        q[ch, i, j, z, quarter] = out[z, j]
            else:
                out = out.reshape(4, 2, 32, 256)
                for j in range(4):
                    for z in range(2):
                        q[ch, i, j, z, quarter] = out[j, z]

    moving = [start_reduce(ch, back_tile, q, q_in1) for ch in range(2)]
    sums = finish_reduce(moving, q, q_in1, q_s1, q_in2, q_s2, q_in3)

    for ch in range(2):
        for quarter in range(2):
            pieces2 = sums[ch][quarter].astype(BF16)
            back[0, ch * 2 + quarter] = pieces2
    swap = []
    for d in (2, 1, 3):
        swap.append(send(back.at[0, (c + d) % 4], back.at[1, c], {"cmp": (c + d) % 4}))
    back[1, c] = back[0, c]
    wait_recv(swap)
    for half in range(2):
        value = jnp.concatenate([back[1, 2 * half], back[1, 2 * half + 1]], axis=1)
        value = jnp.where(pre[half] > 0.0, value.astype(F32), 0.0).astype(BF16)
        gpt[half, first[half], second[half], zh] = value

    g3z = [gather_z(ch, gpt) for ch in range(2)]
    g3s = []
    for ch in range(2):
        g3z[ch].wait_recv()
        g3s.append(gather_second(ch, gpt))
    g3f = []
    for ch in range(2):
        wait_recv(g3s[ch])
        g3f.append(gather_first(ch, gpt))

    g_z.wait_recv()
    g_far = send(gl.at[across_z], gl.at[across_z], {"cmp": across_core})
    for ch in range(2):
        wait_recv(g2f[ch])
    g_core.wait_recv()
    g_far.wait_recv()

    def unit_tile(buf, ch, i):
        if ch == 0:
            parts = [buf[ch, i, j, z] for z in range(2) for j in range(4)]
        else:
            parts = [buf[ch, j, i, z] for z in range(2) for j in range(4)]
        return jnp.concatenate(parts, axis=0)

    for i in range(4):
        tile = jnp.concatenate([unit_tile(h2, 0, i), unit_tile(h2, 1, i)], axis=1)

        @pl.loop(0, 4)
        def _(k):
            cols = pl.ds(pl.multiple_of(k * 512, 512), 512)
            gh[pl.ds(i * 256, 256), cols] = dot(tile, gl[:, :, cols].reshape(1024, 512)).astype(BF16)

        fetch(gh.at[pl.ds(i * 256, 256)], gh_hbm.at[pl.ds(i * 256, 256)])

    for ch in range(2):
        wait_recv(g3f[ch])
    for i in range(4):
        out = dot_t(featt[0], unit_tile(gpt, 0, i)) + dot_t(featt[1], unit_tile(gpt, 1, i))
        gt[:, i * 256 : (i + 1) * 256] = out
    fetch(gt, gt_hbm)
    for copy in local[4:]:
        copy.wait()
    for copy in sent:
        copy.wait_send()


def first_of(ch, x, y):
    return x * (1 - ch) + y * ch


def second_of(ch, x, y):
    return y * (1 - ch) + x * ch


def body(features, w_trunk, w_head, bias_trunk, bias_head, targets, block_mask):
    hbm = pl.BlockSpec(memory_space=pl.ANY)
    vmem = pl.BlockSpec(memory_space=pltpu.VMEM)
    return pl.pallas_call(
        kernel,
        out_shape=(
            jax.ShapeDtypeStruct((512, 1024), F32),
            jax.ShapeDtypeStruct((1024, 2048), BF16),
        ),
        in_specs=[hbm, hbm, hbm, vmem, vmem, hbm, pl.BlockSpec(memory_space=pltpu.SMEM)],
        out_specs=(hbm, hbm),
        scratch_shapes=[
            pltpu.VMEM((4, 4, 2, 4, 32, 2048), BF16),
            pltpu.VMEM((512, 1024), BF16),
            pltpu.VMEM((4, 2, 4, 32, 512), BF16),
            pltpu.VMEM((4, 256, 512), BF16),
            pltpu.VMEM((2, 512, 512), BF16),
            pltpu.VMEM((256, 2048), BF16),
            pltpu.VMEM((2, 4, 4, 2, 32, 512), F32),
            pltpu.VMEM((2, 3, 4, 2, 32, 512), F32),
            pltpu.VMEM((2, 4, 2, 32, 512), F32),
            pltpu.VMEM((2, 3, 2, 32, 512), F32),
            pltpu.VMEM((2, 2, 32, 512), F32),
            pltpu.VMEM((2, 32, 512), F32),
            pltpu.VMEM((2, 32, 512), F32),
            pltpu.VMEM((4, 32, 256), BF16),
            pltpu.VMEM((2, 4, 4, 2, 2, 32, 256), BF16),
            pltpu.VMEM((256, 4096), BF16),
            pltpu.VMEM((2, 4, 4, 2, 32, 512), BF16),
            pltpu.VMEM((4, 256, 2048), BF16),
            pltpu.VMEM((2048, 256), BF16),
            pltpu.VMEM((2, 4, 4, 2, 2, 32, 256), BF16),
            pltpu.VMEM((2, 3, 4, 2, 2, 32, 256), BF16),
            pltpu.VMEM((2, 4, 2, 2, 32, 256), BF16),
            pltpu.VMEM((2, 3, 2, 2, 32, 256), BF16),
            pltpu.VMEM((2, 2, 2, 32, 256), BF16),
            pltpu.VMEM((2, 2, 32, 256), BF16),
            pltpu.VMEM((2, 4, 32, 256), BF16),
            pltpu.VMEM((2, 4, 4, 2, 32, 512), BF16),
            pltpu.VMEM((1024, 2048), BF16),
            pltpu.VMEM((512, 1024), F32),
            pltpu.SemaphoreType.DMA((84,)),
            pltpu.SemaphoreType.DMA((84,)),
            pltpu.SemaphoreType.DMA((9,)),
        ],
        compiler_params=pltpu.CompilerParams(
            collective_id=0, has_side_effects=True, vmem_limit_bytes=62 << 20
        ),
    )(
        features,
        w_trunk,
        w_head.reshape(4, 4, 2, 4, 32, 2048),
        bias_trunk.reshape(32, 128),
        bias_head.reshape(1, 2048),
        targets,
        block_mask,
    )


def solution(mesh):
    return jax.shard_map(
        body,
        mesh=mesh,
        in_specs=(
            P("cmp", "task"),
            P("task", "cmp"),
            P(None, "task"),
            P(),
            P("task"),
            P("cmp", "task"),
            P(),
        ),
        out_specs=(P("task", "cmp"), P("cmp", "task")),
        check_vma=False,
    )
```

```python
import jax
import jax.numpy as jnp
from jax import lax
from jax.experimental import pallas as pl
from jax.experimental.pallas import tpu as pltpu
from jax.sharding import PartitionSpec as P

BLOCK = 512
MESH = pl.DeviceIdType.MESH
BF16 = jnp.bfloat16
F32 = jnp.float32
NEAR, FAR = (0, 1), (2, 3)
COPIES = 150
EARLY = 144


def dot(a, b):
    return jnp.dot(a, b, preferred_element_type=F32)


def dot_t(a, b):
    return lax.dot_general(a, b, (((1,), (1,)), ((), ())), preferred_element_type=F32)


def kernel(
    feat_hbm, wt_hbm, wh_hbm, bt_ref, bh_ref, tg_hbm, mask_ref,
    gt_hbm, gh_hbm,
    wh, wt, wtt, feat, featt, tg,
    p, p_in1, p_s1, p_in2, p_s2, p_in3, pre, pieces,
    h1, h1t, acc, h2n, h2f, gl, glt,
    q, q_in1, q_s1, q_in2, q_s2, q_in3, back, back_in, gpt,
    gh, gt, ssem, rsem, lsem,
):
    c = lax.axis_index("cmp")
    t = lax.axis_index("task")
    x, zh, y = t // 8, (t // 4) % 2, t % 4
    zl, core = c // 2, c % 2
    mate = 1 - core
    to_mate = {"cmp": 2 * zl + mate}
    to_twin = {"cmp": 2 * (1 - zl) + core}
    to_cross = {"cmp": 2 * (1 - zl) + mate}

    first, second = (x, y, x, y), (y, x, y, x)

    def to_first(k, d):
        if k % 2 == 0:
            return {"task": ((x + d) % 4) * 8 + zh * 4 + y}
        return {"task": x * 8 + zh * 4 + (y + d) % 4}

    def to_second(k, d):
        return to_first(k + 1, d)

    to_other_z = {"task": x * 8 + (1 - zh) * 4 + y}

    sent = []

    def send(src, dst, device):
        i = len(sent)
        copy = pltpu.make_async_remote_copy(
            src_ref=src, dst_ref=dst, send_sem=ssem.at[i], recv_sem=rsem.at[i],
            device_id=device, device_id_type=MESH,
        )
        copy.start()
        sent.append(copy)
        return copy

    local = []

    def fetch(src, dst):
        copy = pltpu.make_async_copy(src, dst, lsem.at[len(local)])
        copy.start()
        local.append(copy)
        return copy

    def wait_recv(copies):
        for copy in copies:
            copy.wait_recv()

    get_feat = fetch(feat_hbm, feat.at[core])
    get_wt = fetch(wt_hbm, wt)
    get_tg = fetch(tg_hbm, tg)
    get_wh = fetch(wh_hbm, wh)

    barrier = pltpu.get_barrier_semaphore()
    peers = [to_mate, to_twin, to_cross, to_other_z]
    peers += [to_first(k, d) for k in (0, 1) for d in (1, 2, 3)]
    for peer in peers:
        pl.semaphore_signal(barrier, inc=1, device_id=peer, device_id_type=MESH)
    pl.semaphore_wait(barrier, len(peers))

    get_feat.wait()
    f_twin = send(feat.at[core], feat.at[2 + core], to_twin)
    f_mate = send(feat.at[core], feat.at[core], to_mate)

    def turn_feat(slot):
        featt[slot] = feat[slot].T

    turn_feat(core)
    get_wt.wait()

    @pl.loop(0, 4)
    def _(i):
        block = wt[:, pl.ds(pl.multiple_of(i * 256, 256), 256)].T
        wtt[i] = block.reshape(2, 4, 32, 512)

    f_mate.wait_recv()
    turn_feat(mate)

    def start_sum(slots, tile, buf, arrive):
        copies = {k: [] for k in slots}
        for d in (2, 1, 3, 0):
            for k in slots:
                i = (first[k] + d) % 4
                tile(k, i)
                if d:
                    copies[k].append(send(buf.at[k, i], arrive.at[k, d - 1], to_first(k, d)))
        return copies

    def second_sum(slots, copies, buf, arrive, total, arrive2):
        out = {}
        for k in slots:
            wait_recv(copies[k])

            @pl.loop(0, 4)
            def _(j):
                for z in range(2):
                    value = buf[k, first[k], j, z].astype(F32)
                    for d in range(3):
                        value = value + arrive[k, d, j, z].astype(F32)
                    total[k, j, z] = value.astype(BF16)

            out[k] = [
                send(total.at[k, (second[k] + d) % 4], arrive2.at[k, d - 1], to_second(k, d))
                for d in (2, 1, 3)
            ]
        return out

    def third_sum(slots, copies, total, arrive2, total2, arrive3):
        out = {}
        for k in slots:
            wait_recv(copies[k])
            for z in range(2):
                value = total[k, second[k], z].astype(F32)
                for d in range(3):
                    value = value + arrive2[k, d, z].astype(F32)
                total2[k, z] = value.astype(BF16)
            out[k] = send(total2.at[k], arrive3.at[k], to_other_z)
        return out

    def last_sum(k, copies, total2, arrive3):
        copies[k].wait_recv()
        return [total2[k, z].astype(F32) + arrive3[k, z].astype(F32) for z in range(2)]

    def swap(slots, buf, dst):
        if slots == NEAR:
            return [send(buf.at[mate], dst(core), to_mate)]
        return [
            send(buf.at[2 + core], dst(2 + core), to_twin),
            send(buf.at[2 + mate], dst(2 + core), to_cross),
        ]

    def gather_small(slots, buf, base=0):
        out = {}
        for k in slots:
            part = buf.at[k - base, first[k], second[k]]
            out[k] = [send(part, part, to_second(k, d)) for d in (2, 1, 3)]
        return out

    def gather_large(slots, copies, buf, base=0):
        out = {}
        for k in slots:
            wait_recv(copies[k])
            part = buf.at[k - base, first[k]]
            out[k] = [send(part, part, to_first(k, d)) for d in (1, 3, 2)]
        return out

    def pre_tile(k, i):
        if k % 2 == 0:
            parts = [wtt[i, z, j] for j in range(4) for z in range(2)]
        else:
            parts = [wtt[j, z, i] for j in range(4) for z in range(2)]
        out = dot(jnp.concatenate(parts, axis=0), featt[k])
        p[k, i] = out.astype(BF16).reshape(4, 2, 32, 256)

    def pre_share(slots, copies):
        lane = lax.broadcasted_iota(jnp.int32, (32, 128), 1)
        unit = lax.broadcasted_iota(jnp.int32, (32, 128), 0)
        bias = []
        for z in range(2):
            row = jnp.broadcast_to(bt_ref[pl.ds(c * 8 + 2 * x + z, 1), :], (32, 128))
            column = jnp.where(lane == unit + y * 32, row, 0.0)
            bias.append(jnp.sum(column, axis=1, keepdims=True))
        for k in slots:
            sums = last_sum(k, copies, p_s2, p_in3)
            for z in range(2):
                value = sums[z] + bias[z]
                pre[k, z] = value
                value = jnp.maximum(value, 0.0).astype(BF16)
                pieces[k, z] = value
                if k in FAR:
                    h2f[k - 2, first[k], second[k], z] = value

    def place(parity):
        return x * (1 - parity) + y * parity, y * (1 - parity) + x * parity

    def hidden_slot(k):
        i, j = place(core)
        return h1.at[k, i, j]

    n1 = start_sum(NEAR, pre_tile, p, p_in1)
    f_twin.wait_recv()
    f_far = send(feat.at[2 + core], feat.at[2 + core], to_mate)
    turn_feat(2 + core)
    f_far.wait_recv()
    turn_feat(2 + mate)
    f1 = start_sum(FAR, pre_tile, p, p_in1)
    n2 = second_sum(NEAR, n1, p, p_in1, p_s1, p_in2)
    f2 = second_sum(FAR, f1, p, p_in1, p_s1, p_in2)
    n3 = third_sum(NEAR, n2, p_s1, p_in2, p_s2, p_in3)
    f3 = third_sum(FAR, f2, p_s1, p_in2, p_s2, p_in3)
    pre_share(NEAR, n3)
    n_swap = swap(NEAR, pieces, hidden_slot)
    i, j = place(core)
    for z in range(2):
        h1[core, i, j, z] = pieces[core, z]
    pre_share(FAR, f3)
    f_swap = swap(FAR, pieces, hidden_slot)
    wait_recv(n_swap)
    n_small = gather_small(NEAR, h1)
    wait_recv(f_swap)
    f_small = gather_small(FAR, h1)
    e_small = gather_small(FAR, h2f, 2)
    n_large = gather_large(NEAR, n_small, h1)
    f_large = gather_large(FAR, f_small, h1)

    def turn_hidden(k):
        @pl.loop(0, 4)
        def _(i):
            if k % 2 == 0:
                parts = [h1[k, i, j, z] for z in range(2) for j in range(4)]
            else:
                parts = [h1[k, j, i, z] for z in range(2) for j in range(4)]
            column = pl.multiple_of(k * 1024 + i * 256, 256)
            h1t[:, pl.ds(column, 256)] = jnp.concatenate(parts, axis=0).T

    for k in NEAR:
        wait_recv(n_large[k])
        turn_hidden(k)
    e_large = gather_large(FAR, e_small, h2f, 2)
    h_mate = send(h1.at[mate], h2n.at[core], to_mate)
    h_own = fetch(h1.at[core], h2n.at[core])
    get_wh.wait()

    @pl.loop(0, 4)
    def _(k):
        cols = pl.ds(pl.multiple_of(k * BLOCK, BLOCK), BLOCK)
        weight = wh[pl.ds(2 * zl, 2), :, :, :, :, cols].reshape(2048, BLOCK)
        acc[:, cols] = dot(h1t[:, :2048], weight)

    for k in FAR:
        wait_recv(f_large[k])
        turn_hidden(k)
    get_tg.wait()

    @pl.loop(0, 4)
    def _(k):
        cols = pl.ds(pl.multiple_of(k * BLOCK, BLOCK), BLOCK)
        weight = wh[pl.ds(2 - 2 * zl, 2), :, :, :, :, cols].reshape(2048, BLOCK)
        logits = acc[:, cols] + dot(h1t[:, 2048:], weight) + bh_ref[:, cols]
        seen = mask_ref[zl, t * 4 + k].astype(F32)
        error = seen * (jax.nn.sigmoid(logits) - tg[:, cols].astype(F32)) * (1.0 / 32.0)
        error = error.astype(BF16)
        gl[core, :, cols] = error
        glt[cols, :] = error.T

    parts = (pl.ds(0, EARLY), pl.ds(EARLY, 256 - EARLY))

    def send_errors(part):
        return send(gl.at[core, part], gl.at[2 + core, part], to_twin)

    g_early = send_errors(parts[0])
    g_mate = send(gl.at[core], gl.at[core], to_mate)

    def back_tile(k, i):
        quarter = 2 * (zl if k in NEAR else 1 - zl) + k % 2
        if k % 2 == 0:
            parts = [wh[quarter, i, z, j] for j in range(4) for z in range(2)]
        else:
            parts = [wh[quarter, j, z, i] for j in range(4) for z in range(2)]
        out = dot(jnp.concatenate(parts, axis=0), glt[...])
        q[k, i] = out.astype(BF16).reshape(4, 2, 32, 256)

    def back_share(slots, copies):
        for k in slots:
            sums = last_sum(k, copies, q_s2, q_in3)
            for z in range(2):
                back[k, z] = sums[z].astype(BF16)

    def back_slot(k):
        return back_in.at[k]

    def mask_share(slots):
        for k in slots:
            for z in range(2):
                value = jnp.where(pre[k, z] > 0.0, back_in[k, z].astype(F32), 0.0)
                gpt[k, first[k], second[k], z] = value.astype(BF16)

    n1 = start_sum(NEAR, back_tile, q, q_in1)
    f1 = start_sum(FAR, back_tile, q, q_in1)
    n2 = second_sum(NEAR, n1, q, q_in1, q_s1, q_in2)
    f2 = second_sum(FAR, f1, q, q_in1, q_s1, q_in2)
    n3 = third_sum(NEAR, n2, q_s1, q_in2, q_s2, q_in3)
    f3 = third_sum(FAR, f2, q_s1, q_in2, q_s2, q_in3)
    back_share(NEAR, n3)
    n_swap = swap(NEAR, back, back_slot)
    for z in range(2):
        back_in[core, z] = back[core, z]
    back_share(FAR, f3)
    f_swap = swap(FAR, back, back_slot)
    g_late = send_errors(parts[1])
    wait_recv(n_swap)
    mask_share(NEAR)
    n_small = gather_small(NEAR, gpt)
    wait_recv(f_swap)
    mask_share(FAR)
    f_small = gather_small(FAR, gpt)
    n_large = gather_large(NEAR, n_small, gpt)
    f_large = gather_large(FAR, f_small, gpt)

    g_far = []
    for copy, part in zip((g_early, g_late), parts):
        copy.wait_recv()
        g_far.append(send(gl.at[2 + core, part], gl.at[2 + core, part], to_mate))
    h_own.wait()
    h_mate.wait_recv()
    for k in FAR:
        wait_recv(e_large[k])
    g_mate.wait_recv()
    wait_recv(g_far)

    def chain_tile(buf, k, i, parity):
        parts = []
        for z in range(2):
            for j in range(4):
                a, b = i * (1 - parity) + j * parity, j * (1 - parity) + i * parity
                parts.append(buf[k, a, b, z])
        return jnp.concatenate(parts, axis=0)

    for i in range(4):
        tile = [chain_tile(h2n, k, i, core) for k in NEAR]
        tile += [chain_tile(h2f, k - 2, i, k % 2) for k in FAR]
        tile = jnp.concatenate(tile, axis=1)

        @pl.loop(0, 4)
        def _(k):
            cols = pl.ds(pl.multiple_of(k * 512, 512), 512)
            out = dot(tile, gl[:, :, cols].reshape(1024, 512))
            gh[pl.ds(i * 256, 256), cols] = out.astype(BF16)

        fetch(gh.at[pl.ds(i * 256, 256)], gh_hbm.at[pl.ds(i * 256, 256)])

    for k in NEAR:
        wait_recv(n_large[k])
    for i in range(4):
        out = sum(dot_t(featt[k], chain_tile(gpt, k, i, k % 2)) for k in NEAR)
        gt[:, i * 256 : (i + 1) * 256] = out
    for k in FAR:
        wait_recv(f_large[k])
    for i in range(4):
        out = sum(dot_t(featt[k], chain_tile(gpt, k, i, k % 2)) for k in FAR)
        gt[:, i * 256 : (i + 1) * 256] += out
    fetch(gt, gt_hbm)
    for copy in local[5:]:
        copy.wait()
    for copy in sent:
        copy.wait_send()


def copy_kernel(gt_in, gh_in, gt_out, gh_out, gt, gh, sem):
    ins, outs = [], []
    for src, mid, dst in ((gt_in, gt, gt_out), (gh_in, gh, gh_out)):
        rows = src.shape[0] // 4
        for i in range(4):
            part = pl.ds(i * rows, rows)
            n = len(ins)
            ins.append(pltpu.make_async_copy(src.at[part], mid.at[part], sem.at[0, n]))
            outs.append(pltpu.make_async_copy(mid.at[part], dst.at[part], sem.at[1, n]))
    for copy in ins:
        copy.start()
    for copy, out in zip(ins, outs):
        copy.wait()
        out.start()
    for out in outs:
        out.wait()


def body(features, w_trunk, w_head, bias_trunk, bias_head, targets, block_mask):
    hbm = pl.BlockSpec(memory_space=pl.ANY)
    vmem = pl.BlockSpec(memory_space=pltpu.VMEM)
    outs = (
        jax.ShapeDtypeStruct((512, 1024), F32),
        jax.ShapeDtypeStruct((1024, 2048), BF16),
    )
    chain = (4, 4, 2, 32, 256)
    results = pl.pallas_call(
        kernel,
        out_shape=outs,
        in_specs=[hbm, hbm, hbm, vmem, vmem, hbm, pl.BlockSpec(memory_space=pltpu.SMEM)],
        out_specs=(hbm, hbm),
        scratch_shapes=[
            pltpu.VMEM((4, 4, 2, 4, 32, 2048), BF16),
            pltpu.VMEM((512, 1024), BF16),
            pltpu.VMEM((4, 2, 4, 32, 512), BF16),
            pltpu.VMEM((4, 256, 512), BF16),
            pltpu.VMEM((4, 512, 256), BF16),
            pltpu.VMEM((256, 2048), BF16),
            pltpu.VMEM((4, *chain), BF16),
            pltpu.VMEM((4, 3, 4, 2, 32, 256), BF16),
            pltpu.VMEM((4, 4, 2, 32, 256), BF16),
            pltpu.VMEM((4, 3, 2, 32, 256), BF16),
            pltpu.VMEM((4, 2, 32, 256), BF16),
            pltpu.VMEM((4, 2, 32, 256), BF16),
            pltpu.VMEM((4, 2, 32, 256), F32),
            pltpu.VMEM((4, 2, 32, 256), BF16),
            pltpu.VMEM((4, *chain), BF16),
            pltpu.VMEM((256, 4096), BF16),
            pltpu.VMEM((256, 2048), F32),
            pltpu.VMEM((2, *chain), BF16),
            pltpu.VMEM((2, *chain), BF16),
            pltpu.VMEM((4, 256, 2048), BF16),
            pltpu.VMEM((2048, 256), BF16),
            pltpu.VMEM((4, *chain), BF16),
            pltpu.VMEM((4, 3, 4, 2, 32, 256), BF16),
            pltpu.VMEM((4, 4, 2, 32, 256), BF16),
            pltpu.VMEM((4, 3, 2, 32, 256), BF16),
            pltpu.VMEM((4, 2, 32, 256), BF16),
            pltpu.VMEM((4, 2, 32, 256), BF16),
            pltpu.VMEM((4, 2, 32, 256), BF16),
            pltpu.VMEM((4, 2, 32, 256), BF16),
            pltpu.VMEM((4, *chain), BF16),
            pltpu.VMEM((1024, 2048), BF16),
            pltpu.VMEM((512, 1024), F32),
            pltpu.SemaphoreType.DMA((COPIES,)),
            pltpu.SemaphoreType.DMA((COPIES,)),
            pltpu.SemaphoreType.DMA((10,)),
        ],
        compiler_params=pltpu.CompilerParams(
            collective_id=0, has_side_effects=True, vmem_limit_bytes=62 << 20
        ),
    )(
        features,
        w_trunk,
        w_head.reshape(4, 4, 2, 4, 32, 2048),
        bias_trunk.reshape(32, 128),
        bias_head.reshape(1, 2048),
        targets,
        block_mask,
    )
    return pl.pallas_call(
        copy_kernel,
        out_shape=outs,
        in_specs=[hbm, hbm],
        out_specs=(hbm, hbm),
        scratch_shapes=[
            pltpu.VMEM((512, 1024), F32),
            pltpu.VMEM((1024, 2048), BF16),
            pltpu.SemaphoreType.DMA((2, 8)),
        ],
        compiler_params=pltpu.CompilerParams(vmem_limit_bytes=60 << 20),
    )(*results)


def solution(mesh):
    return jax.shard_map(
        body,
        mesh=mesh,
        in_specs=(
            P("cmp", "task"),
            P("task", "cmp"),
            P(None, "task"),
            P(),
            P("task"),
            P("cmp", "task"),
            P(),
        ),
        out_specs=(P("task", "cmp"), P("cmp", "task")),
        check_vma=False,
    )
```

```python
import jax
import jax.numpy as jnp
from jax import lax
from jax.experimental import pallas as pl
from jax.experimental.pallas import tpu as pltpu
from jax.sharding import PartitionSpec as P

BLOCK = 512
MESH = pl.DeviceIdType.MESH
BF16 = jnp.bfloat16
F32 = jnp.float32
NEAR, FAR, ALL = (0, 1), (2, 3), (0, 1, 2, 3)
HALF = 128
COPIES = 272


def dot(a, b):
    return jnp.dot(a, b, preferred_element_type=F32)


def dot_t(a, b):
    return lax.dot_general(a, b, (((1,), (1,)), ((), ())), preferred_element_type=F32)


def kernel(
    feat_hbm, wt_hbm, wh_hbm, bt_ref, bh_ref, tg_hbm, mask_ref,
    gt_hbm, gh_hbm,
    wh, wt, wtt, feat, featt, tg,
    p, p_in1, p_s1, p_in2, p_s2, p_in3, p_far, pre, pieces,
    h1, h1t, h2n, h2f, gl, glt,
    q, q_in1, q_s1, q_in2, q_s2, q_in3, q_far, back, back_in, gpt,
    gh, gt, ssem, rsem, lsem,
):
    c = lax.axis_index("cmp")
    t = lax.axis_index("task")
    x, zh, y = t // 8, (t // 4) % 2, t % 4
    zl, core = c // 2, c % 2
    mate = 1 - core
    to_mate = {"cmp": 2 * zl + mate}
    to_twin = {"cmp": 2 * (1 - zl) + core}
    to_cross = {"cmp": 2 * (1 - zl) + mate}

    first, second = (x, y, x, y), (y, x, y, x)

    def to_first(k, d):
        if k % 2 == 0:
            return {"task": ((x + d) % 4) * 8 + zh * 4 + y}
        return {"task": x * 8 + zh * 4 + (y + d) % 4}

    def to_second(k, d):
        return to_first(k + 1, d)

    other_z = x * 8 + (1 - zh) * 4 + y
    to_other_z = {"task": other_z}
    to_far = (
        (2 + core, to_twin), (2 + core, {**to_twin, "task": other_z}),
        (2 + mate, to_cross), (2 + mate, {**to_cross, "task": other_z}),
    )

    sent = []

    def send(src, dst, device):
        i = len(sent)
        copy = pltpu.make_async_remote_copy(
            src_ref=src, dst_ref=dst, send_sem=ssem.at[i], recv_sem=rsem.at[i],
            device_id=device, device_id_type=MESH,
        )
        copy.start()
        sent.append(copy)
        return copy

    local = []

    def fetch(src, dst):
        copy = pltpu.make_async_copy(src, dst, lsem.at[len(local)])
        copy.start()
        local.append(copy)
        return copy

    def wait_recv(copies):
        for copy in copies:
            copy.wait_recv()

    get_feat = fetch(feat_hbm, feat.at[core])
    get_wt = fetch(wt_hbm, wt)
    get_tg = fetch(tg_hbm, tg)
    get_wh = fetch(wh_hbm, wh)

    barrier = pltpu.get_barrier_semaphore()
    peers = [to_mate, to_other_z] + [device for _, device in to_far]
    peers += [to_first(k, d) for k in (0, 1) for d in (1, 2, 3)]
    for peer in peers:
        pl.semaphore_signal(barrier, inc=1, device_id=peer, device_id_type=MESH)
    pl.semaphore_wait(barrier, len(peers))

    get_feat.wait()
    halves = [slice(w * HALF, (w + 1) * HALF) for w in range(2)]
    f_twin = [send(feat.at[core, rows], feat.at[2 + core, rows], to_twin) for rows in halves]
    f_mate = send(feat.at[core], feat.at[core], to_mate)

    def turn_feat(slot, rows):
        featt[slot, :, rows] = feat[slot, rows, :].T

    for rows in halves:
        turn_feat(core, rows)
    get_wt.wait()

    @pl.loop(0, 4)
    def _(i):
        block = wt[:, pl.ds(pl.multiple_of(i * 256, 256), 256)].T
        wtt[i] = block.reshape(2, 4, 32, 512)

    f_mate.wait_recv()
    for rows in halves:
        turn_feat(mate, rows)

    def start_sum(slots, tile, buf, arrive, steps=(2, 1, 3, 0)):
        copies = {k: [] for k in slots}
        for d in steps:
            for k in slots:
                i = (first[k] + d) % 4
                tile(k, i)
                if d:
                    copies[k].append(send(buf.at[k, i], arrive.at[k, d - 1], to_first(k, d)))
        return copies

    def second_sum(slots, copies, buf, arrive, total, arrive2):
        out = {}
        for k in slots:
            wait_recv(copies[k])

            @pl.loop(0, 4)
            def _(j):
                for z in range(2):
                    value = buf[k, first[k], j, z].astype(F32)
                    for d in range(3):
                        value = value + arrive[k, d, j, z].astype(F32)
                    total[k, j, z] = value.astype(BF16)

            out[k] = [
                send(total.at[k, (second[k] + d) % 4], arrive2.at[k, d - 1], to_second(k, d))
                for d in (2, 1, 3)
            ]
        return out

    def end_second(slots, copies, total, arrive2, total2):
        for k in slots:
            wait_recv(copies[k])
            for z in range(2):
                value = total[k, second[k], z].astype(F32)
                for d in range(3):
                    value = value + arrive2[k, d, z].astype(F32)
                total2[k, z] = value.astype(BF16)

    def third_sum(slots, total2, arrive3):
        return {k: send(total2.at[k], arrive3.at[k], to_other_z) for k in slots}

    def last_sum(k, copies, total2, arrive3):
        copies[k].wait_recv()
        return [total2[k, z].astype(F32) + arrive3[k, z].astype(F32) for z in range(2)]

    def swap_near(buf, dst):
        return [send(buf.at[mate], dst(core), to_mate)]

    def swap_far(total2, dst):
        return [send(total2.at[k], dst.at[core, zh], device) for k, device in to_far]

    def gather_small(slots, buf, base=0):
        out = {}
        for k in slots:
            part = buf.at[k - base, first[k], second[k]]
            out[k] = [send(part, part, to_second(k, d)) for d in (2, 1, 3)]
        return out

    def gather_large(slots, copies, buf, base=0, steps=(2, 1, 3)):
        out = {}
        for k in slots:
            wait_recv(copies[k])
            out[k] = more_large(k, buf, base, steps)
        return out

    def more_large(k, buf, base, steps):
        part = buf.at[k - base, first[k]]
        return [send(part, part, to_first(k, d)) for d in steps]

    class Wave:
        def __init__(self, bufs, tile, share, buf, dst, far_in, own, place_share, gathered):
            self.parts, self.in1, self.s1, self.in2, self.s2, self.in3 = bufs
            self.tile, self.share, self.buf, self.dst = tile, share, buf, dst
            self.far_in, self.own, self.place_share, self.gathered = far_in, own, place_share, gathered
            self.first = {}

        def sum_first(self, slots):
            self.first.update(start_sum(slots, self.tile, self.parts, self.in1))

        def sum_second(self):
            self.second = second_sum(ALL, self.first, self.parts, self.in1, self.s1, self.in2)

        def sum_third(self):
            end_second(NEAR, self.second, self.s1, self.in2, self.s2)
            self.third = third_sum(NEAR, self.s2, self.in3)
            end_second(FAR, self.second, self.s1, self.in2, self.s2)
            self.far = swap_far(self.s2, self.far_in)

        def third_far(self):
            return third_sum(FAR, self.s2, self.in3)

        def gather_second(self):
            self.share(NEAR, self.third)
            near = swap_near(self.buf, self.dst)
            self.own()
            wait_recv(self.far)
            self.place_share(FAR)
            wait_recv(near)
            self.place_share(NEAR)
            self.small = gather_small(ALL, self.gathered)

        def gather_first(self):
            self.large = gather_large(ALL, self.small, self.gathered)

        def wait(self):
            for k in ALL:
                wait_recv(self.large[k])

    def pre_wave(w):
        parts, in1, s1, in2, s2, in3, from_far, mine, piece, hidden, hidden_far = (
            buf.at[w] for buf in (p, p_in1, p_s1, p_in2, p_s2, p_in3, p_far, pre, pieces, h1, h2f)
        )
        lanes = slice(w * HALF, (w + 1) * HALF)

        def tile(k, i):
            if k % 2 == 0:
                rows = [wtt[i, z, j] for j in range(4) for z in range(2)]
            else:
                rows = [wtt[j, z, i] for j in range(4) for z in range(2)]
            out = dot(jnp.concatenate(rows, axis=0), featt[k, :, lanes])
            parts[k, i] = out.astype(BF16).reshape(4, 2, 32, HALF)

        def share(slots, copies):
            for k in slots:
                sums = last_sum(k, copies, s2, in3)
                for z in range(2):
                    value = sums[z] + bias(c, z)
                    mine[k, z] = value
                    value = jnp.maximum(value, 0.0).astype(BF16)
                    piece[k, z] = value
                    if k in FAR:
                        hidden_far[k - 2, first[k], second[k], z] = value

        def own():
            i, j = place(core)
            for z in range(2):
                hidden[core, i, j, z] = piece[core, z]

        def slot(k):
            i, j = place(core)
            return hidden.at[k, i, j]

        def place_hidden(slots):
            if slots == NEAR:
                return
            for k in FAR:
                for z in range(2):
                    value = from_far[k - 2, 0, z].astype(F32) + from_far[k - 2, 1, z].astype(F32)
                    value = jnp.maximum(value + bias(2 - 2 * zl + k % 2, z), 0.0)
                    hidden[k, first[k], second[k], z] = value.astype(BF16)

        return Wave((parts, in1, s1, in2, s2, in3), tile, share, piece, slot, from_far, own, place_hidden, hidden)

    def bias(quarter, z):
        lane = lax.broadcasted_iota(jnp.int32, (32, 128), 1)
        unit = lax.broadcasted_iota(jnp.int32, (32, 128), 0)
        row = jnp.broadcast_to(bt_ref[pl.ds(quarter * 8 + 2 * x + z, 1), :], (32, 128))
        return jnp.sum(jnp.where(lane == unit + y * 32, row, 0.0), axis=1, keepdims=True)

    def place(parity):
        return x * (1 - parity) + y * parity, y * (1 - parity) + x * parity

    waves = [pre_wave(w) for w in range(2)]
    for wave in waves:
        wave.sum_first(NEAR)
    for wave, copy, rows in zip(waves, f_twin, halves):
        copy.wait_recv()
        f_far = send(feat.at[2 + core, rows], feat.at[2 + core, rows], to_mate)
        turn_feat(2 + core, rows)
        f_far.wait_recv()
        turn_feat(2 + mate, rows)
        wave.sum_first(FAR)
    for wave in waves:
        wave.sum_second()
    for wave in waves:
        wave.sum_third()
    own_far = [wave.third_far() for wave in waves]
    for wave in waves:
        wave.gather_second()
    for wave in waves:
        wave.gather_first()
    e_small = []
    for w in range(2):
        waves[w].share(FAR, own_far[w])
        e_small.append(gather_small(FAR, h2f.at[w], 2))

    def turn_hidden(w):
        for k in ALL:
            @pl.loop(0, 4)
            def _(i):
                if k % 2 == 0:
                    parts = [h1[w, k, i, j, z] for z in range(2) for j in range(4)]
                else:
                    parts = [h1[w, k, j, i, z] for z in range(2) for j in range(4)]
                quarter = 2 * (zl if k in NEAR else 1 - zl) + k % 2
                column = pl.multiple_of(quarter * 1024 + i * 256, 256)
                h1t[w, :, pl.ds(column, 256)] = jnp.concatenate(parts, axis=0).T

    def logit_errors(w):
        rows = slice(w * HALF, (w + 1) * HALF)

        @pl.loop(0, 4)
        def _(k):
            cols = pl.ds(pl.multiple_of(k * BLOCK, BLOCK), BLOCK)
            weight = wh[:, :, :, :, :, cols].reshape(4096, BLOCK)
            logits = dot(h1t[w], weight) + bh_ref[:, cols]
            chance = 0.5 + 0.5 * jnp.tanh(0.5 * logits)
            seen = mask_ref[zl, t * 4 + k].astype(F32)
            error = seen * (chance - tg[rows, cols].astype(F32)) * (1.0 / 32.0)
            error = error.astype(BF16)
            gl[core, rows, cols] = error
            glt[w, cols, :] = error.T

    def back_wave(w):
        parts, in1, s1, in2, s2, in3, from_far, mine, piece, piece_in, grad = (
            buf.at[w] for buf in (q, q_in1, q_s1, q_in2, q_s2, q_in3, q_far, pre, back, back_in, gpt)
        )

        def tile(k, i):
            quarter = 2 * (zl if k in NEAR else 1 - zl) + k % 2
            if k % 2 == 0:
                rows = [wh[quarter, i, z, j] for j in range(4) for z in range(2)]
            else:
                rows = [wh[quarter, j, z, i] for j in range(4) for z in range(2)]
            out = dot(jnp.concatenate(rows, axis=0), glt[w])
            parts[k, i] = out.astype(BF16).reshape(4, 2, 32, HALF)

        def share(slots, copies):
            for k in slots:
                sums = last_sum(k, copies, s2, in3)
                for z in range(2):
                    piece[k, z] = sums[z].astype(BF16)

        def own():
            for z in range(2):
                piece_in[core, z] = piece[core, z]

        def slot(k):
            return piece_in.at[k]

        def mask_share(slots):
            for k in slots:
                for z in range(2):
                    if k in NEAR:
                        value = piece_in[k, z].astype(F32)
                    else:
                        value = from_far[k - 2, 0, z].astype(F32) + from_far[k - 2, 1, z].astype(F32)
                    value = jnp.where(mine[k, z] > 0.0, value, 0.0)
                    grad[k, first[k], second[k], z] = value.astype(BF16)

        return Wave((parts, in1, s1, in2, s2, in3), tile, share, piece, slot, from_far, own, mask_share, grad)

    g_rows, g_twin = [], []

    def send_errors(start, count):
        part = pl.ds(start, count)
        g_rows.append(part)
        g_twin.append(send(gl.at[core, part], gl.at[2 + core, part], to_twin))

    backs = [back_wave(w) for w in range(2)]
    e_large, h_mate, h_own, g_mate = [], [], [], []
    for w in range(2):
        waves[w].wait()
        turn_hidden(w)
        if w == 0:
            get_wh.wait()
            get_tg.wait()
        logit_errors(w)
        if w == 0:
            send_errors(0, HALF)
        else:
            send_errors(HALF, 48)
            backs[0].sum_second()
        backs[w].sum_first(ALL)
        h_mate.append(send(h1.at[w, mate], h2n.at[w, core], to_mate))
        h_own.append(fetch(h1.at[w, core], h2n.at[w, core]))
        part = pl.ds(w * HALF, HALF)
        g_mate.append(send(gl.at[core, part], gl.at[core, part], to_mate))
        if w == 0:
            e_large = [gather_large(FAR, e_small[v], h2f.at[v], 2) for v in range(2)]
    backs[0].sum_third()
    send_errors(HALF + 48, 64)
    backs[1].sum_second()
    backs[1].sum_third()
    send_errors(HALF + 112, 16)
    for wave in backs:
        wave.gather_second()
    for wave in backs:
        wave.gather_first()

    g_far = []
    for copy, part in zip(g_twin, g_rows):
        copy.wait_recv()
        g_far.append(send(gl.at[2 + core, part], gl.at[2 + core, part], to_mate))
    for copy in h_own:
        copy.wait()
    wait_recv(h_mate)
    for copies in e_large:
        for k in FAR:
            wait_recv(copies[k])
    wait_recv(g_mate)
    wait_recv(g_far)

    def chain_tile(buf, k, i, parity):
        parts = []
        for z in range(2):
            for j in range(4):
                a, b = i * (1 - parity) + j * parity, j * (1 - parity) + i * parity
                parts.append(buf[k, a, b, z])
        return jnp.concatenate(parts, axis=0)

    for i in range(4):
        tile = [chain_tile(h2n.at[w], k, i, core) for k in NEAR for w in range(2)]
        tile += [chain_tile(h2f.at[w], k - 2, i, k % 2) for k in FAR for w in range(2)]
        tile = jnp.concatenate(tile, axis=1)

        @pl.loop(0, 4)
        def _(k):
            cols = pl.ds(pl.multiple_of(k * 512, 512), 512)
            out = dot(tile, gl[:, :, cols].reshape(1024, 512))
            gh[pl.ds(i * 256, 256), cols] = out.astype(BF16)

        fetch(gh.at[pl.ds(i * 256, 256)], gh_hbm.at[pl.ds(i * 256, 256)])

    for w in range(2):
        backs[w].wait()
        known = jnp.concatenate([featt[k, :, w * HALF : (w + 1) * HALF] for k in ALL], axis=1)
        for i in range(4):
            cols = slice(i * 256, (i + 1) * 256)
            grad = jnp.concatenate([chain_tile(gpt.at[w], k, i, k % 2) for k in ALL], axis=1)
            if w == 0:
                gt[:, cols] = dot_t(known, grad)
            else:
                gt[:, cols] += dot_t(known, grad)
    fetch(gt, gt_hbm)
    for copy in local[6:]:
        copy.wait()
    for copy in sent:
        copy.wait_send()


def body(features, w_trunk, w_head, bias_trunk, bias_head, targets, block_mask):
    hbm = pl.BlockSpec(memory_space=pl.ANY)
    vmem = pl.BlockSpec(memory_space=pltpu.VMEM)
    outs = (
        jax.ShapeDtypeStruct((512, 1024), F32),
        jax.ShapeDtypeStruct((1024, 2048), BF16),
    )
    chain = (4, 4, 2, 32, HALF)
    return pl.pallas_call(
        kernel,
        out_shape=outs,
        in_specs=[hbm, hbm, hbm, vmem, vmem, hbm, pl.BlockSpec(memory_space=pltpu.SMEM)],
        out_specs=(hbm, hbm),
        scratch_shapes=[
            pltpu.VMEM((4, 4, 2, 4, 32, 2048), BF16),
            pltpu.VMEM((512, 1024), BF16),
            pltpu.VMEM((4, 2, 4, 32, 512), BF16),
            pltpu.VMEM((4, 256, 512), BF16),
            pltpu.VMEM((4, 512, 256), BF16),
            pltpu.VMEM((256, 2048), BF16),
            pltpu.VMEM((2, 4, *chain), BF16),
            pltpu.VMEM((2, 4, 3, 4, 2, 32, HALF), BF16),
            pltpu.VMEM((2, 4, 4, 2, 32, HALF), BF16),
            pltpu.VMEM((2, 4, 3, 2, 32, HALF), BF16),
            pltpu.VMEM((2, 4, 2, 32, HALF), BF16),
            pltpu.VMEM((2, 4, 2, 32, HALF), BF16),
            pltpu.VMEM((2, 2, 2, 2, 32, HALF), BF16),
            pltpu.VMEM((2, 4, 2, 32, HALF), F32),
            pltpu.VMEM((2, 4, 2, 32, HALF), BF16),
            pltpu.VMEM((2, 4, *chain), BF16),
            pltpu.VMEM((2, HALF, 4096), BF16),
            pltpu.VMEM((2, 2, *chain), BF16),
            pltpu.VMEM((2, 2, *chain), BF16),
            pltpu.VMEM((4, 256, 2048), BF16),
            pltpu.VMEM((2, 2048, HALF), BF16),
            pltpu.VMEM((2, 4, *chain), BF16),
            pltpu.VMEM((2, 4, 3, 4, 2, 32, HALF), BF16),
            pltpu.VMEM((2, 4, 4, 2, 32, HALF), BF16),
            pltpu.VMEM((2, 4, 3, 2, 32, HALF), BF16),
            pltpu.VMEM((2, 4, 2, 32, HALF), BF16),
            pltpu.VMEM((2, 4, 2, 32, HALF), BF16),
            pltpu.VMEM((2, 2, 2, 2, 32, HALF), BF16),
            pltpu.VMEM((2, 4, 2, 32, HALF), BF16),
            pltpu.VMEM((2, 4, 2, 32, HALF), BF16),
            pltpu.VMEM((2, 4, *chain), BF16),
            pltpu.VMEM((1024, 2048), BF16),
            pltpu.VMEM((512, 1024), F32),
            pltpu.SemaphoreType.DMA((COPIES,)),
            pltpu.SemaphoreType.DMA((COPIES,)),
            pltpu.SemaphoreType.DMA((11,)),
        ],
        compiler_params=pltpu.CompilerParams(
            collective_id=0, has_side_effects=True, vmem_limit_bytes=62 << 20
        ),
    )(
        features,
        w_trunk,
        w_head.reshape(4, 4, 2, 4, 32, 2048),
        bias_trunk.reshape(32, 128),
        bias_head.reshape(1, 2048),
        targets,
        block_mask,
    )


def solution(mesh):
    return jax.shard_map(
        body,
        mesh=mesh,
        in_specs=(
            P("cmp", "task"),
            P("task", "cmp"),
            P(None, "task"),
            P(),
            P("task"),
            P("cmp", "task"),
            P(),
        ),
        out_specs=(P("task", "cmp"), P("cmp", "task")),
        check_vma=False,
    )
```

```python
import jax
import jax.numpy as jnp
from jax import lax
from jax.experimental import pallas as pl
from jax.experimental.pallas import tpu as pltpu
from jax.sharding import PartitionSpec as P

BLOCK = 512
MESH = pl.DeviceIdType.MESH
BF16 = jnp.bfloat16
F32 = jnp.float32
NEAR, FAR, ALL = (0, 1), (2, 3), (0, 1, 2, 3)
HALF = 128
COPIES = 272


def dot(a, b):
    return jnp.dot(a, b, preferred_element_type=F32)


def dot_t(a, b):
    return lax.dot_general(a, b, (((1,), (1,)), ((), ())), preferred_element_type=F32)


def kernel(
    feat_hbm, wt_hbm, wh_hbm, bt_ref, bh_ref, tg_hbm, mask_ref,
    gt_hbm, gh_hbm,
    wh, wt, wtt, feat, featt, tg,
    p, p_in1, p_s1, p_in2, p_s2, p_in3, p_far, pre, pieces,
    h1, h1t, h2n, h2f, gl, glt,
    q, q_in1, q_s1, q_in2, q_s2, q_in3, q_far, back, back_in, gpt,
    gh, gt, ssem, rsem, lsem,
):
    c = lax.axis_index("cmp")
    t = lax.axis_index("task")
    x, zh, y = t // 8, (t // 4) % 2, t % 4
    zl, core = c // 2, c % 2
    mate = 1 - core
    to_mate = {"cmp": 2 * zl + mate}
    to_twin = {"cmp": 2 * (1 - zl) + core}
    to_cross = {"cmp": 2 * (1 - zl) + mate}

    first, second = (x, y, x, y), (y, x, y, x)

    def to_first(k, d):
        if k % 2 == 0:
            return {"task": ((x + d) % 4) * 8 + zh * 4 + y}
        return {"task": x * 8 + zh * 4 + (y + d) % 4}

    def to_second(k, d):
        return to_first(k + 1, d)

    other_z = x * 8 + (1 - zh) * 4 + y
    to_other_z = {"task": other_z}
    to_far = (
        (2 + core, to_twin), (2 + core, {**to_twin, "task": other_z}),
        (2 + mate, to_cross), (2 + mate, {**to_cross, "task": other_z}),
    )

    sent = []

    def send(src, dst, device):
        i = len(sent)
        copy = pltpu.make_async_remote_copy(
            src_ref=src, dst_ref=dst, send_sem=ssem.at[i], recv_sem=rsem.at[i],
            device_id=device, device_id_type=MESH,
        )
        copy.start()
        sent.append(copy)
        return copy

    local = []

    def fetch(src, dst):
        copy = pltpu.make_async_copy(src, dst, lsem.at[len(local)])
        copy.start()
        local.append(copy)
        return copy

    def wait_recv(copies):
        for copy in copies:
            copy.wait_recv()

    get_feat = fetch(feat_hbm, feat.at[core])
    get_wt = fetch(wt_hbm, wt)
    get_tg = fetch(tg_hbm, tg)
    get_wh = fetch(wh_hbm, wh)

    barrier = pltpu.get_barrier_semaphore()
    peers = [to_mate, to_other_z] + [device for _, device in to_far]
    peers += [to_first(k, d) for k in (0, 1) for d in (1, 2, 3)]
    for peer in peers:
        pl.semaphore_signal(barrier, inc=1, device_id=peer, device_id_type=MESH)
    pl.semaphore_wait(barrier, len(peers))

    get_feat.wait()
    halves = [slice(w * HALF, (w + 1) * HALF) for w in range(2)]
    f_twin = [send(feat.at[core, rows], feat.at[2 + core, rows], to_twin) for rows in halves]
    f_mate = send(feat.at[core], feat.at[core], to_mate)

    def turn_feat(slot, rows):
        featt[slot, :, rows] = feat[slot, rows, :].T

    for rows in halves:
        turn_feat(core, rows)
    get_wt.wait()

    @pl.loop(0, 4)
    def _(i):
        block = wt[:, pl.ds(pl.multiple_of(i * 256, 256), 256)].T
        wtt[i] = block.reshape(2, 4, 32, 512)

    f_mate.wait_recv()
    for rows in halves:
        turn_feat(mate, rows)

    def start_sum(slots, tile, buf, arrive, steps=(2, 1, 3, 0)):
        copies = {k: [] for k in slots}
        for d in steps:
            for k in slots:
                i = (first[k] + d) % 4
                tile(k, i)
                if d:
                    copies[k].append(send(buf.at[k, i], arrive.at[k, d - 1], to_first(k, d)))
        return copies

    def second_sum(slots, copies, buf, arrive, total, arrive2):
        out = {}
        for k in slots:
            wait_recv(copies[k])

            @pl.loop(0, 4)
            def _(j):
                for z in range(2):
                    value = buf[k, first[k], j, z].astype(F32)
                    for d in range(3):
                        value = value + arrive[k, d, j, z].astype(F32)
                    total[k, j, z] = value.astype(BF16)

            out[k] = [
                send(total.at[k, (second[k] + d) % 4], arrive2.at[k, d - 1], to_second(k, d))
                for d in (2, 1, 3)
            ]
        return out

    def end_second(slots, copies, total, arrive2, total2):
        for k in slots:
            wait_recv(copies[k])
            for z in range(2):
                value = total[k, second[k], z].astype(F32)
                for d in range(3):
                    value = value + arrive2[k, d, z].astype(F32)
                total2[k, z] = value.astype(BF16)

    def third_sum(slots, total2, arrive3):
        return {k: send(total2.at[k], arrive3.at[k], to_other_z) for k in slots}

    def last_sum(k, copies, total2, arrive3):
        copies[k].wait_recv()
        return [total2[k, z].astype(F32) + arrive3[k, z].astype(F32) for z in range(2)]

    def swap_near(buf, dst):
        return [send(buf.at[mate], dst(core), to_mate)]

    def swap_far(total2, dst):
        return [send(total2.at[k], dst.at[core, zh], device) for k, device in to_far]

    def gather_small(slots, buf, base=0):
        out = {}
        for k in slots:
            part = buf.at[k - base, first[k], second[k]]
            out[k] = [send(part, part, to_second(k, d)) for d in (2, 1, 3)]
        return out

    def gather_large(slots, copies, buf, base=0, steps=(2, 1, 3)):
        out = {}
        for k in slots:
            wait_recv(copies[k])
            out[k] = more_large(k, buf, base, steps)
        return out

    def more_large(k, buf, base, steps):
        part = buf.at[k - base, first[k]]
        return [send(part, part, to_first(k, d)) for d in steps]

    class Wave:
        def __init__(self, bufs, tile, share, buf, dst, far_in, own, place_share, gathered):
            self.parts, self.in1, self.s1, self.in2, self.s2, self.in3 = bufs
            self.tile, self.share, self.buf, self.dst = tile, share, buf, dst
            self.far_in, self.own, self.place_share, self.gathered = far_in, own, place_share, gathered
            self.first = {}

        def sum_first(self, slots):
            self.first.update(start_sum(slots, self.tile, self.parts, self.in1))

        def sum_second(self):
            self.second = second_sum(ALL, self.first, self.parts, self.in1, self.s1, self.in2)

        def sum_third(self):
            end_second(NEAR, self.second, self.s1, self.in2, self.s2)
            self.third = third_sum(NEAR, self.s2, self.in3)
            end_second(FAR, self.second, self.s1, self.in2, self.s2)
            self.far = swap_far(self.s2, self.far_in)

        def third_far(self):
            return third_sum(FAR, self.s2, self.in3)

        def gather_second(self):
            self.share(NEAR, self.third)
            near = swap_near(self.buf, self.dst)
            self.own()
            wait_recv(self.far)
            self.place_share(FAR)
            wait_recv(near)
            self.place_share(NEAR)
            self.small = gather_small(ALL, self.gathered)

        def gather_first(self):
            self.large = gather_large(ALL, self.small, self.gathered)

        def wait(self):
            for k in ALL:
                wait_recv(self.large[k])

    def pre_wave(w):
        parts, in1, s1, in2, s2, in3, from_far, mine, piece, hidden, hidden_far = (
            buf.at[w] for buf in (p, p_in1, p_s1, p_in2, p_s2, p_in3, p_far, pre, pieces, h1, h2f)
        )
        lanes = slice(w * HALF, (w + 1) * HALF)

        def tile(k, i):
            if k % 2 == 0:
                rows = [wtt[i, z, j] for j in range(4) for z in range(2)]
            else:
                rows = [wtt[j, z, i] for j in range(4) for z in range(2)]
            out = dot(jnp.concatenate(rows, axis=0), featt[k, :, lanes])
            parts[k, i] = out.astype(BF16).reshape(4, 2, 32, HALF)

        def share(slots, copies):
            for k in slots:
                sums = last_sum(k, copies, s2, in3)
                for z in range(2):
                    value = sums[z] + bias(c, z)
                    mine[k, z] = value
                    value = jnp.maximum(value, 0.0).astype(BF16)
                    piece[k, z] = value
                    if k in FAR:
                        hidden_far[k - 2, first[k], second[k], z] = value

        def own():
            i, j = place(core)
            for z in range(2):
                hidden[core, i, j, z] = piece[core, z]

        def slot(k):
            i, j = place(core)
            return hidden.at[k, i, j]

        def place_hidden(slots):
            if slots == NEAR:
                return
            for k in FAR:
                for z in range(2):
                    value = from_far[k - 2, 0, z].astype(F32) + from_far[k - 2, 1, z].astype(F32)
                    value = jnp.maximum(value + bias(2 - 2 * zl + k % 2, z), 0.0)
                    hidden[k, first[k], second[k], z] = value.astype(BF16)

        return Wave((parts, in1, s1, in2, s2, in3), tile, share, piece, slot, from_far, own, place_hidden, hidden)

    def bias(quarter, z):
        lane = lax.broadcasted_iota(jnp.int32, (32, 128), 1)
        unit = lax.broadcasted_iota(jnp.int32, (32, 128), 0)
        row = jnp.broadcast_to(bt_ref[pl.ds(quarter * 8 + 2 * x + z, 1), :], (32, 128))
        return jnp.sum(jnp.where(lane == unit + y * 32, row, 0.0), axis=1, keepdims=True)

    def place(parity):
        return x * (1 - parity) + y * parity, y * (1 - parity) + x * parity

    waves = [pre_wave(w) for w in range(2)]
    for wave in waves:
        wave.sum_first(NEAR)
    for wave, copy, rows in zip(waves, f_twin, halves):
        copy.wait_recv()
        f_far = send(feat.at[2 + core, rows], feat.at[2 + core, rows], to_mate)
        turn_feat(2 + core, rows)
        f_far.wait_recv()
        turn_feat(2 + mate, rows)
        wave.sum_first(FAR)
    for wave in waves:
        wave.sum_second()
    for wave in waves:
        wave.sum_third()
    own_far = [wave.third_far() for wave in waves]
    for wave in waves:
        wave.gather_second()
    for wave in waves:
        wave.gather_first()
    e_small = []
    for w in range(2):
        waves[w].share(FAR, own_far[w])
        e_small.append(gather_small(FAR, h2f.at[w], 2))

    def turn_hidden(w):
        for k in ALL:
            @pl.loop(0, 4)
            def _(i):
                if k % 2 == 0:
                    parts = [h1[w, k, i, j, z] for z in range(2) for j in range(4)]
                else:
                    parts = [h1[w, k, j, i, z] for z in range(2) for j in range(4)]
                quarter = 2 * (zl if k in NEAR else 1 - zl) + k % 2
                column = pl.multiple_of(quarter * 1024 + i * 256, 256)
                h1t[w, :, pl.ds(column, 256)] = jnp.concatenate(parts, axis=0).T

    def logit_errors(w):
        rows = slice(w * HALF, (w + 1) * HALF)

        @pl.loop(0, 4, unroll=2)
        def _(k):
            cols = pl.ds(pl.multiple_of(k * BLOCK, BLOCK), BLOCK)
            weight = wh[:, :, :, :, :, cols].reshape(4096, BLOCK)
            logits = dot(h1t[w], weight) + bh_ref[:, cols]
            chance = 0.5 + 0.5 * jnp.tanh(0.5 * logits)
            seen = mask_ref[zl, t * 4 + k].astype(F32)
            error = seen * (chance - tg[rows, cols].astype(F32)) * (1.0 / 32.0)
            error = error.astype(BF16)
            gl[core, rows, cols] = error
            glt[w, cols, :] = error.T

    def back_wave(w):
        parts, in1, s1, in2, s2, in3, from_far, mine, piece, piece_in, grad = (
            buf.at[w] for buf in (q, q_in1, q_s1, q_in2, q_s2, q_in3, q_far, pre, back, back_in, gpt)
        )

        def tile(k, i):
            quarter = 2 * (zl if k in NEAR else 1 - zl) + k % 2
            if k % 2 == 0:
                rows = [wh[quarter, i, z, j] for j in range(4) for z in range(2)]
            else:
                rows = [wh[quarter, j, z, i] for j in range(4) for z in range(2)]
            out = dot(jnp.concatenate(rows, axis=0), glt[w])
            parts[k, i] = out.astype(BF16).reshape(4, 2, 32, HALF)

        def share(slots, copies):
            for k in slots:
                sums = last_sum(k, copies, s2, in3)
                for z in range(2):
                    piece[k, z] = sums[z].astype(BF16)

        def own():
            for z in range(2):
                piece_in[core, z] = piece[core, z]

        def slot(k):
            return piece_in.at[k]

        def mask_share(slots):
            for k in slots:
                for z in range(2):
                    if k in NEAR:
                        value = piece_in[k, z].astype(F32)
                    else:
                        value = from_far[k - 2, 0, z].astype(F32) + from_far[k - 2, 1, z].astype(F32)
                    value = jnp.where(mine[k, z] > 0.0, value, 0.0)
                    grad[k, first[k], second[k], z] = value.astype(BF16)

        return Wave((parts, in1, s1, in2, s2, in3), tile, share, piece, slot, from_far, own, mask_share, grad)

    g_rows, g_twin = [], []

    def send_errors(start, count):
        part = pl.ds(start, count)
        g_rows.append(part)
        g_twin.append(send(gl.at[core, part], gl.at[2 + core, part], to_twin))

    backs = [back_wave(w) for w in range(2)]
    e_large, h_mate, h_own, g_mate = [], [], [], []
    for w in range(2):
        waves[w].wait()
        turn_hidden(w)
        if w == 0:
            get_wh.wait()
            get_tg.wait()
        logit_errors(w)
        if w == 0:
            send_errors(0, HALF)
        else:
            send_errors(HALF, HALF)
            backs[0].sum_second()
        backs[w].sum_first(ALL)
        h_mate.append(send(h1.at[w, mate], h2n.at[w, core], to_mate))
        h_own.append(fetch(h1.at[w, core], h2n.at[w, core]))
        part = pl.ds(w * HALF, HALF)
        g_mate.append(send(gl.at[core, part], gl.at[core, part], to_mate))
        if w == 0:
            e_large = [gather_large(FAR, e_small[v], h2f.at[v], 2) for v in range(2)]
    backs[0].sum_third()
    backs[1].sum_second()
    backs[1].sum_third()
    for wave in backs:
        wave.gather_second()
    for wave in backs:
        wave.gather_first()

    g_far = []
    for copy, part in zip(g_twin, g_rows):
        copy.wait_recv()
        g_far.append(send(gl.at[2 + core, part], gl.at[2 + core, part], to_mate))
    for copy in h_own:
        copy.wait()
    wait_recv(h_mate)
    for copies in e_large:
        for k in FAR:
            wait_recv(copies[k])
    wait_recv(g_mate)
    wait_recv(g_far)

    def chain_tile(buf, k, i, parity):
        parts = []
        for z in range(2):
            for j in range(4):
                a, b = i * (1 - parity) + j * parity, j * (1 - parity) + i * parity
                parts.append(buf[k, a, b, z])
        return jnp.concatenate(parts, axis=0)

    for i in range(4):
        tile = [chain_tile(h2n.at[w], k, i, core) for k in NEAR for w in range(2)]
        tile += [chain_tile(h2f.at[w], k - 2, i, k % 2) for k in FAR for w in range(2)]
        tile = jnp.concatenate(tile, axis=1)

        @pl.loop(0, 4)
        def _(k):
            cols = pl.ds(pl.multiple_of(k * 512, 512), 512)
            out = dot(tile, gl[:, :, cols].reshape(1024, 512))
            gh[pl.ds(i * 256, 256), cols] = out.astype(BF16)

        fetch(gh.at[pl.ds(i * 256, 256)], gh_hbm.at[pl.ds(i * 256, 256)])

    for w in range(2):
        backs[w].wait()
        known = jnp.concatenate([featt[k, :, w * HALF : (w + 1) * HALF] for k in ALL], axis=1)
        for i in range(4):
            cols = slice(i * 256, (i + 1) * 256)
            grad = jnp.concatenate([chain_tile(gpt.at[w], k, i, k % 2) for k in ALL], axis=1)
            if w == 0:
                gt[:, cols] = dot_t(known, grad)
            else:
                gt[:, cols] += dot_t(known, grad)
    fetch(gt, gt_hbm)
    for copy in local[6:]:
        copy.wait()
    for copy in sent:
        copy.wait_send()


def body(features, w_trunk, w_head, bias_trunk, bias_head, targets, block_mask):
    hbm = pl.BlockSpec(memory_space=pl.ANY)
    vmem = pl.BlockSpec(memory_space=pltpu.VMEM)
    outs = (
        jax.ShapeDtypeStruct((512, 1024), F32),
        jax.ShapeDtypeStruct((1024, 2048), BF16),
    )
    chain = (4, 4, 2, 32, HALF)
    return pl.pallas_call(
        kernel,
        out_shape=outs,
        in_specs=[hbm, hbm, hbm, vmem, vmem, hbm, pl.BlockSpec(memory_space=pltpu.SMEM)],
        out_specs=(hbm, hbm),
        scratch_shapes=[
            pltpu.VMEM((4, 4, 2, 4, 32, 2048), BF16),
            pltpu.VMEM((512, 1024), BF16),
            pltpu.VMEM((4, 2, 4, 32, 512), BF16),
            pltpu.VMEM((4, 256, 512), BF16),
            pltpu.VMEM((4, 512, 256), BF16),
            pltpu.VMEM((256, 2048), BF16),
            pltpu.VMEM((2, 4, *chain), BF16),
            pltpu.VMEM((2, 4, 3, 4, 2, 32, HALF), BF16),
            pltpu.VMEM((2, 4, 4, 2, 32, HALF), BF16),
            pltpu.VMEM((2, 4, 3, 2, 32, HALF), BF16),
            pltpu.VMEM((2, 4, 2, 32, HALF), BF16),
            pltpu.VMEM((2, 4, 2, 32, HALF), BF16),
            pltpu.VMEM((2, 2, 2, 2, 32, HALF), BF16),
            pltpu.VMEM((2, 4, 2, 32, HALF), F32),
            pltpu.VMEM((2, 4, 2, 32, HALF), BF16),
            pltpu.VMEM((2, 4, *chain), BF16),
            pltpu.VMEM((2, HALF, 4096), BF16),
            pltpu.VMEM((2, 2, *chain), BF16),
            pltpu.VMEM((2, 2, *chain), BF16),
            pltpu.VMEM((4, 256, 2048), BF16),
            pltpu.VMEM((2, 2048, HALF), BF16),
            pltpu.VMEM((2, 4, *chain), BF16),
            pltpu.VMEM((2, 4, 3, 4, 2, 32, HALF), BF16),
            pltpu.VMEM((2, 4, 4, 2, 32, HALF), BF16),
            pltpu.VMEM((2, 4, 3, 2, 32, HALF), BF16),
            pltpu.VMEM((2, 4, 2, 32, HALF), BF16),
            pltpu.VMEM((2, 4, 2, 32, HALF), BF16),
            pltpu.VMEM((2, 2, 2, 2, 32, HALF), BF16),
            pltpu.VMEM((2, 4, 2, 32, HALF), BF16),
            pltpu.VMEM((2, 4, 2, 32, HALF), BF16),
            pltpu.VMEM((2, 4, *chain), BF16),
            pltpu.VMEM((1024, 2048), BF16),
            pltpu.VMEM((512, 1024), F32),
            pltpu.SemaphoreType.DMA((COPIES,)),
            pltpu.SemaphoreType.DMA((COPIES,)),
            pltpu.SemaphoreType.DMA((11,)),
        ],
        compiler_params=pltpu.CompilerParams(
            collective_id=0, has_side_effects=True, vmem_limit_bytes=62 << 20
        ),
    )(
        features,
        w_trunk,
        w_head.reshape(4, 4, 2, 4, 32, 2048),
        bias_trunk.reshape(32, 128),
        bias_head.reshape(1, 2048),
        targets,
        block_mask,
    )


def solution(mesh):
    return jax.shard_map(
        body,
        mesh=mesh,
        in_specs=(
            P("cmp", "task"),
            P("task", "cmp"),
            P(None, "task"),
            P(),
            P("task"),
            P("cmp", "task"),
            P(),
        ),
        out_specs=(P("task", "cmp"), P("cmp", "task")),
        check_vma=False,
    )
```
